512 devices in a mesh: seq: 64 (over z, y), chan: 8 (over x, core).
Axes of the slice: x: 4, y: 4, z: 16, core: 2. Of those that a mesh axis runs over, the one named last changes fastest.
Arguments:
- query: bfloat16 [8192, 4096], P('seq', 'chan'), may hold values from -6 to 6
- key: bfloat16 [8192, 4096], P('seq', 'chan'), may hold values from -6 to 6
- value: bfloat16 [8192, 4096], P('seq', 'chan'), may hold values from -6 to 6
- residual: bfloat16 [8192, 4096], P('seq', 'chan'), may hold values from -6 to 6
- short_taps: float32 [3, 3, 4096], P(None, None, 'chan'), may hold values from -3.5 to 3.5
- decay: float32 [16, 4096], P(None, 'chan'), may hold values from 0.00012207031 to 0.05
- residue: float32 [16, 4096], P(None, 'chan'), may hold values from -3 to 3
- skip_gain: float32 [4096], P('chan'), may hold values from 0.5 to 1.5
- segments: int32 [64], replicated, may hold values from 0 to 7, never falling along the last dimension, each value on 1 to 32 neighbouring positions
- out_weight: bfloat16 [4096, 4096], P('seq', 'chan'), may hold values from -0.09375 to 0.09375
Outputs:
- block_out: bfloat16 [8192, 4096], P('seq', 'chan')
The draws below stay inside these ranges and needn't reach their ends.
Inputs may be any that keep to these rules, and one draw needn't show every extreme that they name: `segments`: contig ids of the tiles never fall; each contig covers 1 to 32 tiles, one exactly 32.
All inputs are finite; a program needn't handle non-finite values.
Results may differ from the reference program's by a relative error of at most 0.0063.
Values may be sent and summed in bfloat16 or wider, within the bound.
A program may use at most 64 MiB of HBM per device.

```python
import math
import jax
import jax.numpy as jnp
import numpy as np
from jax import lax

D = 4096
MODES = 16
SHORT = 3
TILE = 128
CONTIGS = 8
SEQ_LEN = 8192
TILES = 64
MOST = 32


def shard_levels(stream_key, extent, cuts, least, largest):
    loudness = 1.0
    for axis_at, blocks in cuts:
        heights = jax.random.uniform(jax.random.fold_in(jax.random.fold_in(stream_key, 6), axis_at), (blocks,), jnp.float32, least / len(cuts), largest / len(cuts))
        loudness = loudness * jnp.repeat(jnp.exp(heights), extent[axis_at] // blocks).reshape((-1,) + (1,) * (len(extent) - 1 - axis_at))
    return loudness


def length_profile(number_of, total, limit, lean):
    loads = [(1 << 20) // math.isqrt(standing ** lean) + 1 for standing in range(2, number_of + 1)]
    rest, given = total - limit - (number_of - 1), [1] * (number_of - 1)
    while rest > 0:
        candidates = [i for i in range(number_of - 1) if given[i] < limit]
        pool, left = sum([loads[i] for i in candidates]), rest
        for i in candidates:
            more = min(limit - given[i], max(1, left * loads[i] // pool), rest)
            given[i] = given[i] + more
            rest = rest - more
    return np.array([limit] + given)


def ragged_sizes(stream_key, amount, total, most, slope):
    if amount == 2:
        one = jax.random.randint(stream_key, (), max(1, total - most), min(most, total - 1) + 1)
        return jnp.stack([one, total - one])
    sizes = jnp.asarray(length_profile(amount, total, most, slope), jnp.int32)
    couples = (amount - 1) // 2
    donor, receiver = sizes[1:1 + 2 * couples:2], sizes[2:2 + 2 * couples:2]
    room = jnp.minimum(donor - 1, most - receiver)
    shifted = jax.random.randint(jax.random.fold_in(stream_key, 1), (couples,), 0, 1 << 20) % (room + 1)
    sizes = sizes.at[1:1 + 2 * couples:2].set(donor - shifted).at[2:2 + 2 * couples:2].set(receiver + shifted)
    return sizes[jax.random.permutation(jax.random.fold_in(stream_key, 2), amount)]


def gaussian(rng, dims, spread, most, cuts=(), kind=jnp.bfloat16):
    loudness = shard_levels(rng, dims, cuts, -0.22, 0.18) if cuts else 1.0
    drawn = jax.random.normal(rng, dims, jnp.float32) * spread * loudness
    return jnp.minimum(jnp.maximum(drawn, -most), most).astype(kind)


def setup_inputs(seed: int = 0) -> dict:
    keys = jax.random.split(jax.random.key(seed), 11)
    query = gaussian(keys[0], (SEQ_LEN, D), 1.0, 6.0, ((0, 64), (1, 8)))
    key = gaussian(keys[1], (SEQ_LEN, D), 1.0, 6.0, ((0, 64), (1, 8)))
    value = gaussian(keys[2], (SEQ_LEN, D), 1.0, 6.0, ((0, 64), (1, 8)))
    residual = gaussian(keys[3], (SEQ_LEN, D), 1.0, 6.0, ((0, 64), (1, 8)))
    short_taps = gaussian(keys[4], (3, SHORT, D), SHORT ** -0.5, 3.5, ((2, 8),), jnp.float32)
    decay = jnp.clip(jnp.exp(math.log(0.05) - 6.015181 * jax.random.uniform(keys[5], (MODES, D), jnp.float32) ** shard_levels(keys[5], (MODES, D), ((1, 8),), -0.2, 0.2)), 0.00012207031, 0.05)
    residue = gaussian(keys[6], (MODES, D), 0.5, 3.0, ((1, 8),), jnp.float32)
    skip_gain = jnp.clip(0.5 + 1.0 * jax.random.uniform(keys[7], (D,), jnp.float32) ** shard_levels(keys[7], (D,), ((0, 8),), -0.2, 0.2), 0.5, 1.5)
    segments = jnp.searchsorted(jnp.cumsum(ragged_sizes(keys[8], CONTIGS, TILES, MOST, 2)), jnp.arange(TILES), side="right").astype(jnp.int32)
    out_weight = gaussian(keys[9], (D, D), D ** -0.5, 0.09375, ((0, 64), (1, 8)))
    return dict(query=query, key=key, value=value, residual=residual, short_taps=short_taps, decay=decay, residue=residue, skip_gain=skip_gain, segments=segments, out_weight=out_weight)


def pair_combine(earlier, later):
    return (earlier[0] * later[0], later[0] * earlier[1] + later[1])

def phase_one(blocks, same, decay, gain):
    width, count, tile = blocks.shape
    steps = jnp.arange(tile, dtype=jnp.float32)
    table = jnp.einsum('mc,mct->ct', gain, jnp.exp(-decay[:, :, None] * steps), precision=lax.Precision.HIGHEST)
    places = jnp.arange(tile, dtype=jnp.int32)
    lagged = places[:, None] - places[None, :]
    toeplitz = jnp.where(lagged[None] >= 0, table[:, jnp.clip(lagged, 0, tile - 1)], jnp.float32(0.0))
    inside = jnp.einsum('cts,cbs->cbt', toeplitz, blocks, precision=lax.Precision.HIGH)
    tail = jnp.exp(-decay[:, :, None] * (tile - 1 - steps))
    local = jnp.einsum('mcs,cbs->bmc', tail, blocks, precision=lax.Precision.HIGH)
    factor = jnp.exp(-decay * tile)[None] * same[:, None, None]
    cums, states = lax.associative_scan(pair_combine, (factor, local), axis=0)
    return (inside, states, cums)

def phase_two(inside, states, cums, carry, same, decay, gain, skip, blocks):
    tile = blocks.shape[2]
    steps = jnp.arange(tile, dtype=jnp.float32)
    ending = states + cums * carry[None]
    entering = jnp.concatenate([carry[None], ending[:-1]], axis=0)
    reach = gain[:, :, None] * jnp.exp(-decay[:, :, None] * (steps + 1.0))
    cross = jnp.einsum('mct,bmc->cbt', reach, entering, precision=lax.Precision.HIGHEST)
    return inside + cross * same[None, :, None] + skip[:, None, None] * blocks

def short_mix(stream, taps, segments):
    length = stream.shape[0]
    padded = jnp.concatenate([jnp.zeros((SHORT - 1, stream.shape[1]), jnp.float32), stream.astype(jnp.float32)], axis=0)
    places = jnp.arange(length, dtype=jnp.int32)
    own = segments[places // TILE]
    total = jnp.zeros(stream.shape, jnp.float32)
    for tap in range(SHORT):
        earlier = places - tap
        other = segments[jnp.clip(earlier, 0, length - 1) // TILE]
        live = (earlier >= 0) & (other == own)
        moved = padded[SHORT - 1 - tap:SHORT - 1 - tap + length]
        total = total + jnp.where(live[:, None], moved * taps[tap][None, :], jnp.float32(0.0))
    return total

def reference(query, key, value, residual, short_taps, decay, residue, skip_gain, segments, out_weight):
    length, width = query.shape
    group = min(512, width)
    count = width // group
    blocks_all = length // TILE
    same = jnp.concatenate([jnp.zeros((1,), jnp.float32), (segments[1:] == segments[:-1]).astype(jnp.float32)])

    def split(array):
        return jnp.moveaxis(array.reshape(array.shape[0], count, group), 1, 0)

    def one_group(inputs):
        q_part, k_part, v_part, taps, rate, weight, skip = inputs
        q_mixed = short_mix(q_part, taps[0], segments)
        k_mixed = short_mix(k_part, taps[1], segments)
        v_mixed = short_mix(v_part, taps[2], segments)
        mixed_input = (k_mixed * v_mixed).astype(jnp.bfloat16)
        gain = weight * jnp.sqrt(rate)
        blocks = mixed_input.astype(jnp.float32).T.reshape(group, blocks_all, TILE)
        inside, states, cums = phase_one(blocks, same, rate, gain)
        carry = jnp.zeros((rate.shape[0], group), jnp.float32)
        long_out = phase_two(inside, states, cums, carry, same, rate, gain, skip, blocks)
        long_rows = long_out.reshape(group, length).astype(jnp.bfloat16).T
        return (q_mixed * long_rows.astype(jnp.float32)).astype(jnp.bfloat16)
    taps_split = jnp.moveaxis(short_taps.reshape(3, SHORT, count, group), 2, 0)
    gated = lax.map(one_group, (split(query), split(key), split(value), taps_split, split(decay), split(residue), skip_gain.reshape(count, group)))
    gated = jnp.moveaxis(gated, 0, 1).reshape(length, width)
    projected = jnp.dot(gated, out_weight, preferred_element_type=jnp.float32)
    return (residual.astype(jnp.float32) + projected).astype(jnp.bfloat16)
```

```python
import jax
import jax.numpy as jnp
from jax import lax
from jax.experimental import pallas as pl
from jax.experimental.pallas import tpu as pltpu
from jax.sharding import PartitionSpec as P

MESH = pl.DeviceIdType.MESH
BF = jnp.bfloat16
F32 = jnp.float32

NZ, NY, NX = 16, 4, 4
TILE = 128
MODES = 16
CH = 128
ROWS = NY * TILE
CHUNK = ROWS // 8
BACK = 8

W_FIRST = ((4, 12), (-4, 4), (8, 8), (1, 15), (-1, 1), (2, 14))
W_NEXT = ((4, 1), (8, 1), (12, 1), (4, -1), (8, -1), (12, -1), (4, 2), (4, -2), (8, -2))


def kernel(
    seg_ref, q_ref, k_ref, v_ref, res_ref, taps_ref, decay_ref, residue_ref, skip_ref, w_ref,
    out_ref,
    stage, rbuf, rim, fq, fk, fv, prm, xs, qs, ys, dtab, gtab, atab, ctab, asend, arecv,
    gbuf, xbuf, wbuf, psend, precv, own,
    y_send, y_recv, rim_send, rim_recv, a_send, a_recv, x_send, x_recv, f_send, f_recv,
    w_send, w_recv, p_send, p_recv,
):
    seq = lax.axis_index("seq")
    chan = lax.axis_index("chan")
    z, y = seq // NY, seq % NY
    x, core = chan // 2, chan % 2

    def dev(dz=0, dy=0, dx=0, dc=0, toy=None):
        yy = lax.rem(y + dy + NY, NY) if toy is None else toy
        return (
            lax.rem(z + dz + NZ, NZ) * NY + yy,
            lax.rem(x + dx + NX, NX) * 2 + (core if dc == 0 else 1 - core),
        )

    barrier = pltpu.get_barrier_semaphore()

    def greet(where):
        pl.semaphore_signal(barrier, inc=1, device_id=where, device_id_type=MESH)

    for j in range(1, NY):
        greet(dev(dy=j))
    for j in range(1, NZ):
        greet(dev(dz=j))
    for j in range(1, NX):
        greet(dev(dx=j))
    greet(dev(dc=1))

    @pl.when(y == NY - 1)
    def _():
        for t in range(NY - 1):
            greet(dev(dz=1, toy=t))

    @pl.when(y != NY - 1)
    def _():
        greet(dev(dz=-1, toy=NY - 1))

    src = lax.broadcasted_iota(jnp.int32, (512, 512), 0)
    dst = lax.broadcasted_iota(jnp.int32, (512, 512), 1)
    wanted = ((dst >> 6) & 1) * 256 + (dst >> 7) * 64 + (dst & 63)
    perm = jnp.where(src == wanted, 1.0, 0.0).astype(BF)
    for s, ref in enumerate((q_ref, k_ref, v_ref)):
        moved = jnp.dot(ref[...], perm, preferred_element_type=F32).astype(BF)
        for t in range(NY):
            stage[t, s] = moved[:, t * CH : (t + 1) * CH]

    pl.semaphore_wait(barrier, 22 + jnp.where(y == NY - 1, 3, 1))

    y_copies = []
    for j in range(1, NY):
        to = lax.rem(y + j, NY)
        cp = pltpu.make_async_remote_copy(
            src_ref=stage.at[to], dst_ref=rbuf.at[y], send_sem=y_send.at[j - 1],
            recv_sem=y_recv.at[j - 1], device_id=dev(dy=j), device_id_type=MESH)
        cp.start()
        y_copies.append(cp)

    def rim_copy(t):
        return pltpu.make_async_remote_copy(
            src_ref=stage.at[t, :, pl.ds(TILE - 16, 16), :], dst_ref=rim, send_sem=rim_send.at[t],
            recv_sem=rim_recv, device_id=dev(dz=1, toy=t), device_id_type=MESH)

    @pl.when(y == NY - 1)
    def _():
        for t in range(NY):
            rim_copy(t).start()

    w_copies = []

    def send_w(source, tile, dz, number):
        cp = pltpu.make_async_remote_copy(
            src_ref=source, dst_ref=wbuf.at[tile], send_sem=w_send.at[len(w_copies)],
            recv_sem=w_recv.at[number], device_id=dev(dz=dz), device_id_type=MESH)
        cp.start()
        w_copies.append(cp)

    def wait_w(number):
        tile = lax.rem(z + number, NZ)
        pltpu.make_async_remote_copy(
            src_ref=w_ref, dst_ref=wbuf.at[tile], send_sem=w_send.at[0],
            recv_sem=w_recv.at[number], device_id=dev(dz=1), device_id_type=MESH).wait_recv()

    for dz, number in W_FIRST:
        send_w(w_ref, z, dz, number)
    wbuf[z] = w_ref[...]

    prm[0:16] = decay_ref[...]
    prm[16:32] = residue_ref[...]
    for s in range(3):
        prm[32 + 3 * s : 35 + 3 * s] = taps_ref[s]
    prm[41:42] = skip_ref[...]
    prm[42:48] = jnp.zeros((6, 512), F32)
    lane = lax.broadcasted_iota(jnp.int32, (512, CH), 1)
    row = lax.broadcasted_iota(jnp.int32, (512, CH), 0)
    pick = jnp.where(row == ((lane >> 6) & 1) * 256 + y * 64 + (lane & 63), 1.0, 0.0).astype(F32)
    mine = jnp.dot(
        prm[...], pick, precision=lax.Precision.HIGHEST, preferred_element_type=F32)
    rate = mine[0:16]
    gain = mine[16:32] * jnp.sqrt(rate)
    taps = [[jnp.broadcast_to(mine[32 + 3 * s + j : 33 + 3 * s + j], (8, CH)) for j in range(3)]
            for s in range(3)]
    skip = jnp.broadcast_to(mine[41:42], (8, CH))

    one = jnp.float32(1.0)
    zero = jnp.float32(0.0)
    seg = [seg_ref[z * NY + t] for t in range(NY)]
    before = seg_ref[jnp.maximum(z * NY - 1, 0)]
    same = [jnp.where(jnp.logical_and(z > 0, before == seg[0]), one, zero)]
    for t in range(1, NY):
        same.append(jnp.where(seg[t] == seg[t - 1], one, zero))
    ends = [jnp.where(seg[t] == seg[NY - 1], one, zero) for t in range(NY)]
    starts = [jnp.where(seg[t] == seg[0], one, zero) for t in range(NY)]
    sub = lax.broadcasted_iota(jnp.int32, (8, CH), 0)

    def by_tile(values):
        total = jnp.full((8, CH), values[0], F32)
        for t in range(1, NY):
            total = jnp.where((sub >> 1) == t, values[t], total)
        return total

    joined = jnp.where((sub & 1) == 1, one, by_tile(same))
    subf = sub.astype(F32)
    rate8 = jnp.broadcast_to(rate[:, None, :], (MODES, 8, CH))
    gain8 = jnp.broadcast_to(gain[:, None, :], (MODES, 8, CH))
    dtab[...] = jnp.exp(-rate8)
    gtab[...] = gain8
    atab[...] = jnp.exp(-rate8 * (CHUNK * (7.0 - subf))[None]) * by_tile(ends)[None]
    ctab[...] = gain8 * jnp.exp(-rate8 * (CHUNK * subf)[None]) * by_tile(starts)[None]
    chunk_decay = jnp.exp(-rate8 * float(CHUNK)) * joined[None]

    streams = (fq, fk, fv)
    here = pl.multiple_of(8 + y * TILE, 8)
    for s in range(3):
        streams[s][pl.ds(here, TILE)] = stage[y, s].astype(F32)
    for j in range(1, NY):
        y_copies[j - 1].wait_recv()
        origin = lax.rem(y - j + NY, NY)
        at = pl.multiple_of(8 + origin * TILE, 8)
        for s in range(3):
            streams[s][pl.ds(at, TILE)] = rbuf[origin, s].astype(F32)
    rim_copy(0).wait_recv()
    for s in range(3):
        streams[s][0:8] = rim[s].astype(F32)[8:16]

    def load(s, b):
        return streams[s][pl.ds(8 + b, 8, stride=CHUNK), :]

    def mix(now, last, older):
        out = []
        for s in range(3):
            out.append(now[s] * taps[s][0] + last[s] * taps[s][1] + older[s] * taps[s][2])
        return out[0], (out[1] * out[2]).astype(BF).astype(F32)

    def keep(b, mixed):
        qs[b] = mixed[0]
        xs[b] = mixed[1]
        return mixed[1]

    m2 = [load(s, -2) * joined for s in range(3)]
    m1 = [load(s, -1) * joined for s in range(3)]
    f0 = [load(s, 0) for s in range(3)]
    f1 = [load(s, 1) for s in range(3)]
    d16 = dtab[...]
    x0 = keep(0, mix(f0, m1, m2))
    x1 = keep(1, mix(f1, f0, m1))
    h = x0[None] * d16 + x1[None]

    def first_pass(b, carry):
        h, last, older = carry
        now = [load(s, b) for s in range(3)]
        xb = keep(b, mix(now, last, older))
        return (h * dtab[...] + xb[None], now, last)

    h, _, _ = lax.fori_loop(2, CHUNK, first_pass, (h, f1, f0), unroll=2)

    asend[...] = jnp.sum(h * atab[...], axis=1).astype(BF)
    a_copies = []
    for k in range(1, BACK + 1):
        cp = pltpu.make_async_remote_copy(
            src_ref=asend, dst_ref=arecv.at[k - 1], send_sem=a_send.at[k - 1],
            recv_sem=a_recv.at[k - 1], device_id=dev(dz=k), device_id_type=MESH)
        cp.start()
        a_copies.append(cp)

    span = 1
    factor = chunk_decay
    state = h
    while span < 8:
        state = state + jnp.where(sub[None] >= span, factor * pltpu.roll(state, span, 1), zero)
        factor = factor * pltpu.roll(factor, span, 1)
        span *= 2
    entering = jnp.where(sub[None] >= 1, pltpu.roll(state, 1, 1) * joined[None], zero)

    def second_pass(b, h):
        xb = xs[b]
        h = h * dtab[...] + xb[None]
        ys[b] = skip * xb + jnp.sum(h * gtab[...], axis=0)
        return h

    lax.fori_loop(0, CHUNK, second_pass, entering, unroll=2)

    for number in (4, 8, 12):
        wait_w(number)
    for number, dz in W_NEXT:
        tile = lax.rem(z + number, NZ)
        send_w(wbuf.at[tile], tile, dz, (number - dz) % NZ)

    carried = jnp.zeros((MODES, CH), F32)
    for k in range(1, BACK + 1):
        a_copies[k - 1].wait_recv()
        ending = seg_ref[jnp.maximum((z - k) * NY + NY - 1, 0)]
        live = jnp.where(jnp.logical_and(z >= k, ending == seg[0]), one, zero)
        weight = jnp.exp(-rate * float(ROWS * (k - 1))) * live
        carried = carried + weight * arecv[k - 1].astype(F32)

    def third_pass(b, e):
        e = e * dtab[...]
        long_out = (ys[b] + jnp.sum(e, axis=0)).astype(BF).astype(F32)
        gbuf[pl.ds(b, 8, stride=CHUNK), :] = qs[b] * long_out
        return e

    lax.fori_loop(0, CHUNK, third_pass, ctab[...] * carried[:, None, :], unroll=2)
    xbuf[chan] = gbuf[...].astype(BF)

    x_copies = []
    for i, move in enumerate((dict(dx=1), dict(dx=-1), dict(dx=2), dict(dc=1))):
        cp = pltpu.make_async_remote_copy(
            src_ref=xbuf.at[chan], dst_ref=xbuf.at[chan], send_sem=x_send.at[i],
            recv_sem=x_recv.at[i], device_id=dev(**move), device_id_type=MESH)
        cp.start()
        x_copies.append(cp)
    f_copies = []
    for i, dx in enumerate((-1, 1, 2)):
        x_copies[i].wait_recv()
        slot = lax.rem(x + dx + NX, NX) * 2 + core
        cp = pltpu.make_async_remote_copy(
            src_ref=xbuf.at[slot], dst_ref=xbuf.at[slot], send_sem=f_send.at[i],
            recv_sem=f_recv.at[i], device_id=dev(dc=1), device_id_type=MESH)
        cp.start()
        f_copies.append(cp)
    x_copies[3].wait_recv()
    for cp in f_copies:
        cp.wait_recv()
    for number in range(1, NZ):
        if number not in (4, 8, 12):
            wait_w(number)

    def project(at):
        rows = pl.ds(pl.multiple_of(at * TILE, TILE), TILE)
        total = jnp.zeros((TILE, 512), F32)
        for p in range(NX):
            left = jnp.concatenate([xbuf[2 * p, rows], xbuf[2 * p + 1, rows]], axis=1)
            right = wbuf[4 * p : 4 * p + 4].reshape(256, 512)
            total = total + jnp.dot(left, right, preferred_element_type=F32)
        return total

    p_copies = []
    for j in range(1, NY):
        psend[j - 1] = project(lax.rem(y + j, NY)).astype(BF)
        cp = pltpu.make_async_remote_copy(
            src_ref=psend.at[j - 1], dst_ref=precv.at[j - 1], send_sem=p_send.at[j - 1],
            recv_sem=p_recv.at[j - 1], device_id=dev(dy=j), device_id_type=MESH)
        cp.start()
        p_copies.append(cp)
    own[...] = project(y) + res_ref[...].astype(F32)
    for j in range(NY - 1):
        p_copies[j].wait_recv()
    out_ref[...] = (
        own[...] + precv[0].astype(F32) + precv[1].astype(F32) + precv[2].astype(F32)
    ).astype(BF)

    for cp in y_copies + w_copies + a_copies + x_copies + f_copies + p_copies:
        cp.wait_send()

    @pl.when(y == NY - 1)
    def _():
        for t in range(NY):
            rim_copy(t).wait_send()


def per_device(
    query, key, value, residual, short_taps, decay, residue, skip_gain, segments, out_weight
):
    vmem = pl.BlockSpec(memory_space=pltpu.VMEM)
    smem = pl.BlockSpec(memory_space=pltpu.SMEM)
    dma = pltpu.SemaphoreType.DMA
    scratch = [
        pltpu.VMEM((NY, 3, TILE, CH), BF),
        pltpu.VMEM((NY, 3, TILE, CH), BF),
        pltpu.VMEM((3, 16, CH), BF),
        pltpu.VMEM((8 + ROWS, CH), F32),
        pltpu.VMEM((8 + ROWS, CH), F32),
        pltpu.VMEM((8 + ROWS, CH), F32),
        pltpu.VMEM((48, 512), F32),
        pltpu.VMEM((CHUNK, 8, CH), F32),
        pltpu.VMEM((CHUNK, 8, CH), F32),
        pltpu.VMEM((CHUNK, 8, CH), F32),
        pltpu.VMEM((MODES, 8, CH), F32),
        pltpu.VMEM((MODES, 8, CH), F32),
        pltpu.VMEM((MODES, 8, CH), F32),
        pltpu.VMEM((MODES, 8, CH), F32),
        pltpu.VMEM((MODES, CH), BF),
        pltpu.VMEM((BACK, MODES, CH), BF),
        pltpu.VMEM((ROWS, CH), F32),
        pltpu.VMEM((2 * NX, ROWS, CH), BF),
        pltpu.VMEM((NZ, 64, 512), BF),
        pltpu.VMEM((NY - 1, TILE, 512), BF),
        pltpu.VMEM((NY - 1, TILE, 512), BF),
        pltpu.VMEM((TILE, 512), F32),
        dma((3,)), dma((3,)), dma((NY,)), dma,
        dma((BACK,)), dma((BACK,)), dma((4,)), dma((4,)), dma((3,)), dma((3,)),
        dma((15,)), dma((NZ,)), dma((3,)), dma((3,)),
    ]
    return pl.pallas_call(
        kernel,
        out_shape=jax.ShapeDtypeStruct((TILE, 512), BF),
        in_specs=[smem] + [vmem] * 9,
        out_specs=vmem,
        scratch_shapes=scratch,
        compiler_params=pltpu.CompilerParams(
            collective_id=0, has_side_effects=True, vmem_limit_bytes=32 * 1024 * 1024),
        name="hyena_block",
    )(segments, query, key, value, residual, short_taps, decay, residue,
      skip_gain.reshape(1, -1), out_weight)


def solution(mesh):
    placed = (
        P("seq", "chan"), P("seq", "chan"), P("seq", "chan"), P("seq", "chan"),
        P(None, None, "chan"), P(None, "chan"), P(None, "chan"), P("chan"), P(),
        P("seq", "chan"),
    )
    return jax.shard_map(
        per_device, mesh=mesh, in_specs=placed, out_specs=P("seq", "chan"), check_vma=False
    )
```

```python
import jax
import jax.numpy as jnp
from jax import lax
from jax.experimental import pallas as pl
from jax.experimental.pallas import tpu as pltpu
from jax.sharding import PartitionSpec as P

MESH = pl.DeviceIdType.MESH
BF = jnp.bfloat16
F32 = jnp.float32

NZ, NY, NX = 16, 4, 4
TILE = 128
MODES = 16
CH = 128
ROWS = NY * TILE
CHUNK = ROWS // 8
BACK = 8

W_FIRST = ((4, 12), (-4, 4), (8, 8), (1, 15), (-1, 1), (2, 14))
W_NEXT = ((4, 1), (8, 1), (12, 1), (4, -1), (8, -1), (12, -1), (4, 2), (4, -2), (8, -2))


def kernel(
    seg_ref, q_hbm, k_hbm, v_hbm, res_hbm, taps_hbm, decay_hbm, residue_hbm, skip_hbm, w_hbm,
    out_ref,
    q_ref, k_ref, v_ref, res_ref, taps_ref, decay_ref, residue_ref, skip_ref, w_ref,
    stage, rbuf, rim, fq, fk, fv, prm, xs, qs, ys, dtab, gtab, atab, ctab, asend, arecv,
    gbuf, xbuf, wbuf, psend, precv, own,
    y_send, y_recv, rim_send, rim_recv, a_send, a_recv, x_send, x_recv, f_send, f_recv,
    w_send, w_recv, p_send, p_recv, in_sem, go, zgo,
):
    inputs = [
        pltpu.make_async_copy(there, ref, in_sem.at[i])
        for i, (there, ref) in enumerate((
            (q_hbm, q_ref), (k_hbm, k_ref), (v_hbm, v_ref), (w_hbm, w_ref), (decay_hbm, decay_ref),
            (residue_hbm, residue_ref), (taps_hbm, taps_ref), (skip_hbm, skip_ref),
            (res_hbm, res_ref)))
    ]
    for cp in inputs:
        cp.start()

    seq = lax.axis_index("seq")
    chan = lax.axis_index("chan")
    z, y = seq // NY, seq % NY
    x, core = chan // 2, chan % 2

    def dev(dz=0, dy=0, dx=0, dc=0, toy=None):
        yy = lax.rem(y + dy + NY, NY) if toy is None else toy
        return (
            lax.rem(z + dz + NZ, NZ) * NY + yy,
            lax.rem(x + dx + NX, NX) * 2 + (core if dc == 0 else 1 - core),
        )

    barrier = pltpu.get_barrier_semaphore()
    hub = jnp.logical_and(chan == 0, y == 0)
    hub_pair = jnp.logical_and(chan == 1, y == 0)

    def greet(sem, where):
        pl.semaphore_signal(sem, inc=1, device_id=where, device_id_type=MESH)

    arecv[...] = jnp.zeros_like(arecv)
    rim[...] = jnp.zeros_like(rim)

    @pl.when(hub)
    def _():
        for j in range(NZ):
            greet(barrier, dev(dz=j, dc=1))

    @pl.when(jnp.logical_not(hub))
    def _():
        greet(barrier, (z * NY, 0))
        for j in range(1, NZ):
            greet(barrier, dev(dz=j))

    @pl.when(y != NY - 1)
    def _():
        greet(barrier, dev(dz=-1, toy=NY - 1))

    src = lax.broadcasted_iota(jnp.int32, (512, 512), 0)
    dst = lax.broadcasted_iota(jnp.int32, (512, 512), 1)
    wanted = ((dst >> 6) & 1) * 256 + (dst >> 7) * 64 + (dst & 63)
    perm = jnp.where(src == wanted, 1.0, 0.0).astype(BF)
    for s, ref in enumerate((q_ref, k_ref, v_ref)):
        inputs[s].wait()
        moved = jnp.dot(ref[...], perm, preferred_element_type=F32).astype(BF)
        for t in range(NY):
            stage[t, s] = moved[:, t * CH : (t + 1) * CH]

    def send_w(source, tile, dz, number):
        at = (number - 1) % NZ
        pltpu.make_async_remote_copy(
            src_ref=source, dst_ref=wbuf.at[tile], send_sem=w_send.at[at],
            recv_sem=w_recv.at[number], device_id=dev(dz=dz), device_id_type=MESH).start()

    def await_w(number):
        return pltpu.make_async_remote_copy(
            src_ref=w_ref, dst_ref=wbuf.at[lax.rem(z + number, NZ)], send_sem=w_send.at[number - 1],
            recv_sem=w_recv.at[number], device_id=dev(dz=1), device_id_type=MESH)

    def planes(moves):
        @pl.when(jnp.logical_not(hub))
        def _():
            pl.semaphore_wait(
                barrier, 15 + jnp.where(hub_pair, 16, jnp.where(y == NY - 1, 3, 0)))

        @pl.when(hub_pair)
        def _():
            greet(zgo, dev(dc=1))

        @pl.when(hub)
        def _():
            pl.semaphore_wait(zgo, 1)

        for dz, number in moves:
            send_w(w_ref, z, dz, number)

    def next_tiles(moves):
        for dz, number in moves:
            send_w(w_ref, z, dz, number)
        for number in (4, 8, 12):
            await_w(number).wait_recv()
        for number, dz in W_NEXT:
            tile = lax.rem(z + number, NZ)
            send_w(wbuf.at[tile], tile, dz, (number - dz) % NZ)

    late = z >= NZ // 2
    inputs[3].wait()

    @pl.when(hub)
    def _():
        pl.semaphore_wait(barrier, NY * 2 * NX - 1)
        for j in range(NY * 2 * NX - 1, 0, -1):
            greet(go, (z * NY + j // (2 * NX), j % (2 * NX)))

    @pl.when(late)
    def _():
        planes(W_FIRST)

    @pl.when(jnp.logical_not(hub))
    def _():
        pl.semaphore_wait(go, 1)

    y_copies = []
    for j in range(1, NY):
        to = lax.rem(y + j, NY)
        cp = pltpu.make_async_remote_copy(
            src_ref=stage.at[to], dst_ref=rbuf.at[y], send_sem=y_send.at[j - 1],
            recv_sem=y_recv.at[j - 1], device_id=dev(dy=j), device_id_type=MESH)
        cp.start()
        y_copies.append(cp)

    def rim_copy(t):
        return pltpu.make_async_remote_copy(
            src_ref=stage.at[t, :, pl.ds(TILE - 16, 16), :], dst_ref=rim, send_sem=rim_send.at[t],
            recv_sem=rim_recv, device_id=dev(dz=1, toy=t), device_id_type=MESH)

    @pl.when(jnp.logical_not(late))
    def _():
        planes(W_FIRST[:3])

    @pl.when(jnp.logical_and(y == NY - 1, z < NZ - 1))
    def _():
        for t in range(NY):
            rim_copy(t).start()

    wbuf[z] = w_ref[...]

    for cp in inputs[4:]:
        cp.wait()
    prm[0:16] = decay_ref[...]
    prm[16:32] = residue_ref[...]
    for s in range(3):
        prm[32 + 3 * s : 35 + 3 * s] = taps_ref[s]
    prm[41:42] = skip_ref[...]
    prm[42:48] = jnp.zeros((6, 512), F32)
    lane = lax.broadcasted_iota(jnp.int32, (512, CH), 1)
    row = lax.broadcasted_iota(jnp.int32, (512, CH), 0)
    pick = jnp.where(row == ((lane >> 6) & 1) * 256 + y * 64 + (lane & 63), 1.0, 0.0).astype(F32)
    mine = jnp.dot(
        prm[...], pick, precision=lax.Precision.HIGHEST, preferred_element_type=F32)
    rate = mine[0:16]
    gain = mine[16:32] * jnp.sqrt(rate)
    taps = [[jnp.broadcast_to(mine[32 + 3 * s + j : 33 + 3 * s + j], (8, CH)) for j in range(3)]
            for s in range(3)]
    skip = jnp.broadcast_to(mine[41:42], (8, CH))

    one = jnp.float32(1.0)
    zero = jnp.float32(0.0)
    seg = [seg_ref[z * NY + t] for t in range(NY)]
    before = seg_ref[jnp.maximum(z * NY - 1, 0)]
    same = [jnp.where(jnp.logical_and(z > 0, before == seg[0]), one, zero)]
    for t in range(1, NY):
        same.append(jnp.where(seg[t] == seg[t - 1], one, zero))
    ends = [jnp.where(seg[t] == seg[NY - 1], one, zero) for t in range(NY)]
    starts = [jnp.where(seg[t] == seg[0], one, zero) for t in range(NY)]
    sub = lax.broadcasted_iota(jnp.int32, (8, CH), 0)

    def by_tile(values):
        total = jnp.full((8, CH), values[0], F32)
        for t in range(1, NY):
            total = jnp.where((sub >> 1) == t, values[t], total)
        return total

    joined = jnp.where((sub & 1) == 1, one, by_tile(same))
    subf = sub.astype(F32)
    rate8 = jnp.broadcast_to(rate[:, None, :], (MODES, 8, CH))
    gain8 = jnp.broadcast_to(gain[:, None, :], (MODES, 8, CH))
    dtab[...] = jnp.exp(-rate8)
    gtab[...] = gain8
    atab[...] = jnp.exp(-rate8 * (CHUNK * (7.0 - subf))[None]) * by_tile(ends)[None]
    ctab[...] = gain8 * jnp.exp(-rate8 * (CHUNK * subf)[None]) * by_tile(starts)[None]
    chunk_decay = jnp.exp(-rate8 * float(CHUNK)) * joined[None]

    streams = (fq, fk, fv)
    here = pl.multiple_of(8 + y * TILE, 8)
    for s in range(3):
        streams[s][pl.ds(here, TILE)] = stage[y, s].astype(F32)
    for j in range(1, NY):
        y_copies[j - 1].wait_recv()
        origin = lax.rem(y - j + NY, NY)
        at = pl.multiple_of(8 + origin * TILE, 8)
        for s in range(3):
            streams[s][pl.ds(at, TILE)] = rbuf[origin, s].astype(F32)
    @pl.when(z > 0)
    def _():
        rim_copy(0).wait_recv()

    for s in range(3):
        streams[s][0:8] = rim[s].astype(F32)[8:16]

    def load(s, b):
        return streams[s][pl.ds(8 + b, 8, stride=CHUNK), :]

    def mix(now, last, older):
        out = []
        for s in range(3):
            out.append(now[s] * taps[s][0] + last[s] * taps[s][1] + older[s] * taps[s][2])
        return out[0], (out[1] * out[2]).astype(BF).astype(F32)

    def keep(b, mixed):
        qs[b] = mixed[0]
        xs[b] = mixed[1]
        return mixed[1]

    m2 = [load(s, -2) * joined for s in range(3)]
    m1 = [load(s, -1) * joined for s in range(3)]
    f0 = [load(s, 0) for s in range(3)]
    f1 = [load(s, 1) for s in range(3)]
    d16 = dtab[...]
    x0 = keep(0, mix(f0, m1, m2))
    x1 = keep(1, mix(f1, f0, m1))
    h = x0[None] * d16 + x1[None]

    def first_pass(b, carry):
        h, last, older = carry
        now = [load(s, b) for s in range(3)]
        xb = keep(b, mix(now, last, older))
        return (h * dtab[...] + xb[None], now, last)

    h, _, _ = lax.fori_loop(2, CHUNK, first_pass, (h, f1, f0), unroll=2)

    asend[...] = jnp.sum(h * atab[...], axis=1).astype(BF)
    a_copies = []
    for k in range(1, BACK + 1):
        cp = pltpu.make_async_remote_copy(
            src_ref=asend, dst_ref=arecv.at[k - 1], send_sem=a_send.at[k - 1],
            recv_sem=a_recv.at[k - 1], device_id=dev(dz=k), device_id_type=MESH)
        a_copies.append(cp)

    for k in range(1, BACK + 1):
        @pl.when(z + k < NZ)
        def _():
            a_copies[k - 1].start()


    span = 1
    factor = chunk_decay
    state = h
    while span < 8:
        state = state + jnp.where(sub[None] >= span, factor * pltpu.roll(state, span, 1), zero)
        factor = factor * pltpu.roll(factor, span, 1)
        span *= 2
    entering = jnp.where(sub[None] >= 1, pltpu.roll(state, 1, 1) * joined[None], zero)

    def second_pass(b, h):
        xb = xs[b]
        h = h * dtab[...] + xb[None]
        ys[b] = skip * xb + jnp.sum(h * gtab[...], axis=0)
        return h

    lax.fori_loop(0, CHUNK, second_pass, entering, unroll=2)

    @pl.when(late)
    def _():
        next_tiles(())

    carried = jnp.zeros((MODES, CH), F32)
    for k in range(1, BACK + 1):
        @pl.when(z >= k)
        def _():
            a_copies[k - 1].wait_recv()

        ending = seg_ref[jnp.maximum((z - k) * NY + NY - 1, 0)]
        live = jnp.where(jnp.logical_and(z >= k, ending == seg[0]), one, zero)
        weight = jnp.exp(-rate * float(ROWS * (k - 1))) * live
        carried = carried + weight * arecv[k - 1].astype(F32)

    def third_pass(b, e):
        e = e * dtab[...]
        long_out = (ys[b] + jnp.sum(e, axis=0)).astype(BF).astype(F32)
        gbuf[pl.ds(b, 8, stride=CHUNK), :] = qs[b] * long_out
        return e

    lax.fori_loop(0, CHUNK, third_pass, ctab[...] * carried[:, None, :], unroll=2)
    xbuf[chan] = gbuf[...].astype(BF)

    x_copies = []
    for i, move in enumerate((dict(dx=1), dict(dx=-1), dict(dx=2), dict(dc=1))):
        cp = pltpu.make_async_remote_copy(
            src_ref=xbuf.at[chan], dst_ref=xbuf.at[chan], send_sem=x_send.at[i],
            recv_sem=x_recv.at[i], device_id=dev(**move), device_id_type=MESH)
        cp.start()
        x_copies.append(cp)
    @pl.when(jnp.logical_not(late))
    def _():
        next_tiles(W_FIRST[3:])

    f_copies = []
    for i, dx in enumerate((-1, 1, 2)):
        x_copies[i].wait_recv()
        slot = lax.rem(x + dx + NX, NX) * 2 + core
        cp = pltpu.make_async_remote_copy(
            src_ref=xbuf.at[slot], dst_ref=xbuf.at[slot], send_sem=f_send.at[i],
            recv_sem=f_recv.at[i], device_id=dev(dc=1), device_id_type=MESH)
        cp.start()
        f_copies.append(cp)
    x_copies[3].wait_recv()
    for cp in f_copies:
        cp.wait_recv()
    for number in range(1, NZ):
        if number not in (4, 8, 12):
            await_w(number).wait_recv()

    def project(at):
        rows = pl.ds(pl.multiple_of(at * TILE, TILE), TILE)
        total = jnp.zeros((TILE, 512), F32)
        for p in range(NX):
            left = jnp.concatenate([xbuf[2 * p, rows], xbuf[2 * p + 1, rows]], axis=1)
            right = wbuf[4 * p : 4 * p + 4].reshape(256, 512)
            total = total + jnp.dot(left, right, preferred_element_type=F32)
        return total

    p_copies = []
    for j in range(1, NY):
        psend[j - 1] = project(lax.rem(y + j, NY)).astype(BF)
        cp = pltpu.make_async_remote_copy(
            src_ref=psend.at[j - 1], dst_ref=precv.at[j - 1], send_sem=p_send.at[j - 1],
            recv_sem=p_recv.at[j - 1], device_id=dev(dy=j), device_id_type=MESH)
        cp.start()
        p_copies.append(cp)
    own[...] = project(y) + res_ref[...].astype(F32)
    for j in range(NY - 1):
        p_copies[j].wait_recv()
    out_ref[...] = (
        own[...] + precv[0].astype(F32) + precv[1].astype(F32) + precv[2].astype(F32)
    ).astype(BF)

    for cp in y_copies + x_copies + f_copies + p_copies:
        cp.wait_send()
    for number in range(1, NZ):
        await_w(number).wait_send()
    for k in range(1, BACK + 1):
        @pl.when(z + k < NZ)
        def _():
            a_copies[k - 1].wait_send()

    @pl.when(jnp.logical_and(y == NY - 1, z < NZ - 1))
    def _():
        for t in range(NY):
            rim_copy(t).wait_send()


def per_device(
    query, key, value, residual, short_taps, decay, residue, skip_gain, segments, out_weight
):
    vmem = pl.BlockSpec(memory_space=pltpu.VMEM)
    hbm = pl.BlockSpec(memory_space=pltpu.HBM)
    smem = pl.BlockSpec(memory_space=pltpu.SMEM)
    dma = pltpu.SemaphoreType.DMA
    scratch = [
        pltpu.VMEM((TILE, 512), BF),
        pltpu.VMEM((TILE, 512), BF),
        pltpu.VMEM((TILE, 512), BF),
        pltpu.VMEM((TILE, 512), BF),
        pltpu.VMEM((3, 3, 512), F32),
        pltpu.VMEM((MODES, 512), F32),
        pltpu.VMEM((MODES, 512), F32),
        pltpu.VMEM((1, 512), F32),
        pltpu.VMEM((64, 512), BF),
        pltpu.VMEM((NY, 3, TILE, CH), BF),
        pltpu.VMEM((NY, 3, TILE, CH), BF),
        pltpu.VMEM((3, 16, CH), BF),
        pltpu.VMEM((8 + ROWS, CH), F32),
        pltpu.VMEM((8 + ROWS, CH), F32),
        pltpu.VMEM((8 + ROWS, CH), F32),
        pltpu.VMEM((48, 512), F32),
        pltpu.VMEM((CHUNK, 8, CH), F32),
        pltpu.VMEM((CHUNK, 8, CH), F32),
        pltpu.VMEM((CHUNK, 8, CH), F32),
        pltpu.VMEM((MODES, 8, CH), F32),
        pltpu.VMEM((MODES, 8, CH), F32),
        pltpu.VMEM((MODES, 8, CH), F32),
        pltpu.VMEM((MODES, 8, CH), F32),
        pltpu.VMEM((MODES, CH), BF),
        pltpu.VMEM((BACK, MODES, CH), BF),
        pltpu.VMEM((ROWS, CH), F32),
        pltpu.VMEM((2 * NX, ROWS, CH), BF),
        pltpu.VMEM((NZ, 64, 512), BF),
        pltpu.VMEM((NY - 1, TILE, 512), BF),
        pltpu.VMEM((NY - 1, TILE, 512), BF),
        pltpu.VMEM((TILE, 512), F32),
        dma((3,)), dma((3,)), dma((NY,)), dma,
        dma((BACK,)), dma((BACK,)), dma((4,)), dma((4,)), dma((3,)), dma((3,)),
        dma((15,)), dma((NZ,)), dma((3,)), dma((3,)), dma((9,)),
        pltpu.SemaphoreType.REGULAR, pltpu.SemaphoreType.REGULAR,
    ]
    return pl.pallas_call(
        kernel,
        out_shape=jax.ShapeDtypeStruct((TILE, 512), BF),
        in_specs=[smem] + [hbm] * 9,
        out_specs=vmem,
        scratch_shapes=scratch,
        compiler_params=pltpu.CompilerParams(
            collective_id=0, has_side_effects=True, vmem_limit_bytes=60 * 1024 * 1024),
        name="hyena_block",
    )(segments, query, key, value, residual, short_taps, decay, residue,
      skip_gain.reshape(1, -1), out_weight)


def solution(mesh):
    placed = (
        P("seq", "chan"), P("seq", "chan"), P("seq", "chan"), P("seq", "chan"),
        P(None, None, "chan"), P(None, "chan"), P(None, "chan"), P("chan"), P(),
        P("seq", "chan"),
    )
    return jax.shard_map(
        per_device, mesh=mesh, in_specs=placed, out_specs=P("seq", "chan"), check_vma=False
    )
```

```python
import jax
import jax.numpy as jnp
from jax import lax
from jax.experimental import pallas as pl
from jax.experimental.pallas import tpu as pltpu
from jax.sharding import PartitionSpec as P

MESH = pl.DeviceIdType.MESH
BF = jnp.bfloat16
F32 = jnp.float32

NZ, NY, NX = 16, 4, 4
TILE = 128
MODES = 16
CH = 128
ROWS = NY * TILE
CHUNK = ROWS // 8
BACK = 8

STEPS = (
    ((0, (2, -2, 1, -1)),),
    ((14, (2, 1)), (2, (-2, -1))),
    ((12, (2, 1)), (4, (-2, -1))),
    ((10, (2, 1)), (6, (-1,))),
)
LATE = {1: (1,), 2: (2,), 3: (3,)}
EARLY = {1: (1,), 3: (2,), 4: (3,)}


def kernel(
    seg_ref, q_hbm, k_hbm, v_hbm, res_hbm, taps_hbm, decay_hbm, residue_hbm, skip_hbm, w_hbm,
    out_ref,
    qkv, res_ref, taps_ref, decay_ref, residue_ref, skip_ref, w_ref,
    stage, rbuf, rim, fq, fk, fv, prm, xs, qs, ys, dtab, gtab, atab, ctab, asend, arecv,
    gbuf, xbuf, wbuf, psend, precv, own, sums,
    y_send, y_recv, rim_send, rim_recv, a_send, a_recv, x_send, x_recv, f_send, f_recv,
    w_send, w_recv, p_send, p_recv, in_sem, go, zgo, blocks, plane,
):
    inputs = [
        pltpu.make_async_copy(there, ref, in_sem.at[i])
        for i, (there, ref) in enumerate((
            (q_hbm, qkv.at[0:TILE]), (k_hbm, qkv.at[TILE : 2 * TILE]),
            (v_hbm, qkv.at[2 * TILE : 3 * TILE]), (w_hbm, w_ref), (decay_hbm, decay_ref),
            (residue_hbm, residue_ref), (taps_hbm, taps_ref), (skip_hbm, skip_ref),
            (res_hbm, res_ref)))
    ]
    for cp in inputs:
        cp.start()

    seq = lax.axis_index("seq")
    chan = lax.axis_index("chan")
    z, y = seq // NY, seq % NY
    x, core = chan // 2, chan % 2

    def dev(dz=0, dy=0, dx=0, dc=0, toy=None):
        yy = lax.rem(y + dy + NY, NY) if toy is None else toy
        return (
            lax.rem(z + dz + NZ, NZ) * NY + yy,
            lax.rem(x + dx + NX, NX) * 2 + (core if dc == 0 else 1 - core),
        )

    barrier = pltpu.get_barrier_semaphore()
    hub = y == 0
    hub_pair = y == 1

    def greet(sem, where):
        pl.semaphore_signal(sem, inc=1, device_id=where, device_id_type=MESH)

    arecv[...] = jnp.zeros_like(arecv)
    rim[...] = jnp.zeros_like(rim)

    @pl.when(hub)
    def _():
        for j in range(1, 2 * NX):
            greet(barrier, (z * NY, lax.rem(chan + j, 2 * NX)))
        for j in range(NZ):
            greet(barrier, dev(dz=j, toy=1))

    @pl.when(jnp.logical_not(hub))
    def _():
        greet(barrier, dev(toy=0))
        for j in range(1, NZ):
            greet(barrier, dev(dz=j))

    @pl.when(y != NY - 1)
    def _():
        greet(barrier, dev(dz=-1, toy=NY - 1))

    def send_w(source, tile, dz, number):
        at = (number - 1) % NZ
        pltpu.make_async_remote_copy(
            src_ref=source, dst_ref=wbuf.at[tile], send_sem=w_send.at[at],
            recv_sem=w_recv.at[number], device_id=dev(dz=dz), device_id_type=MESH).start()

    def await_w(number):
        return pltpu.make_async_remote_copy(
            src_ref=w_ref, dst_ref=wbuf.at[lax.rem(z + number, NZ)], send_sem=w_send.at[number - 1],
            recv_sem=w_recv.at[number], device_id=dev(dz=1), device_id_type=MESH)

    def planes():
        @pl.when(jnp.logical_not(hub))
        def _():
            pl.semaphore_wait(
                barrier, 15 + jnp.where(hub_pair, 16, jnp.where(y == NY - 1, 3, 0)))

        @pl.when(hub_pair)
        def _():
            greet(zgo, dev(toy=0))

        @pl.when(hub)
        def _():
            pl.semaphore_wait(zgo, 1)

    late = z >= NZ // 2
    waited = [number for step in STEPS for number, _ in step if number]

    def pass_on(step):
        for number, moves in STEPS[step]:
            tile = lax.rem(z + number, NZ)
            if number:
                await_w(number).wait_recv()
            for dz in moves:
                send_w(wbuf.at[tile] if number else w_ref, tile, dz, (number - dz) % NZ)

    def w_place(place):
        for when, steps in ((late, LATE), (jnp.logical_not(late), EARLY)):
            if place in steps:
                @pl.when(when)
                def _():
                    for step in steps[place]:
                        pass_on(step)

    src = lax.broadcasted_iota(jnp.int32, (512, 512), 0)
    dst = lax.broadcasted_iota(jnp.int32, (512, 512), 1)
    wanted = ((dst >> 6) & 1) * 256 + (dst >> 7) * 64 + (dst & 63)
    perm = jnp.where(src == wanted, 1.0, 0.0).astype(BF)

    @pl.when(hub)
    def _():
        pl.semaphore_wait(barrier, NY - 1 + 2 * NX - 1)
        for j in range(1, NY):
            greet(go, dev(toy=j))
        for j in range(1, 2 * NX):
            greet(blocks, (z * NY, lax.rem(chan + j, 2 * NX)))

    for i in range(4):
        inputs[i].wait()
    moved = jnp.dot(qkv[...], perm, preferred_element_type=F32).astype(BF)
    for s in range(3):
        for t in range(NY):
            stage[t, s] = moved[s * TILE : (s + 1) * TILE, t * CH : (t + 1) * CH]

    @pl.when(late)
    def _():
        planes()
        pass_on(0)

    @pl.when(jnp.logical_not(hub))
    def _():
        pl.semaphore_wait(go, 1)

    y_copies = []
    for j in range(1, NY):
        to = lax.rem(y + j, NY)
        cp = pltpu.make_async_remote_copy(
            src_ref=stage.at[to], dst_ref=rbuf.at[y], send_sem=y_send.at[j - 1],
            recv_sem=y_recv.at[j - 1], device_id=dev(dy=j), device_id_type=MESH)
        cp.start()
        y_copies.append(cp)

    def rim_copy(t):
        return pltpu.make_async_remote_copy(
            src_ref=stage.at[t, :, pl.ds(TILE - 16, 16), :], dst_ref=rim, send_sem=rim_send.at[t],
            recv_sem=rim_recv, device_id=dev(dz=1, toy=t), device_id_type=MESH)

    @pl.when(jnp.logical_not(late))
    def _():
        planes()
        pass_on(0)

    @pl.when(jnp.logical_and(y == NY - 1, z < NZ - 1))
    def _():
        for t in range(NY):
            rim_copy(t).start()

    @pl.when(hub)
    def _():
        pl.semaphore_wait(blocks, 2 * NX - 1)
        for j in range(1, NY):
            greet(plane, dev(toy=j))

    @pl.when(jnp.logical_not(hub))
    def _():
        pl.semaphore_wait(plane, 1)

    wbuf[z] = w_ref[...]

    for cp in inputs[4:]:
        cp.wait()
    prm[0:16] = decay_ref[...]
    prm[16:32] = residue_ref[...]
    for s in range(3):
        prm[32 + 3 * s : 35 + 3 * s] = taps_ref[s]
    prm[41:42] = skip_ref[...]
    prm[42:48] = jnp.zeros((6, 512), F32)
    lane = lax.broadcasted_iota(jnp.int32, (512, CH), 1)
    row = lax.broadcasted_iota(jnp.int32, (512, CH), 0)
    pick = jnp.where(row == ((lane >> 6) & 1) * 256 + y * 64 + (lane & 63), 1.0, 0.0).astype(F32)
    mine = jnp.dot(
        prm[...], pick, precision=lax.Precision.HIGHEST, preferred_element_type=F32)
    rate = mine[0:16]
    gain = mine[16:32] * jnp.sqrt(rate)
    taps = [[jnp.broadcast_to(mine[32 + 3 * s + j : 33 + 3 * s + j], (8, CH)) for j in range(3)]
            for s in range(3)]
    skip = jnp.broadcast_to(mine[41:42], (8, CH))

    one = jnp.float32(1.0)
    zero = jnp.float32(0.0)
    seg = [seg_ref[z * NY + t] for t in range(NY)]
    before = seg_ref[jnp.maximum(z * NY - 1, 0)]
    same = [jnp.where(jnp.logical_and(z > 0, before == seg[0]), one, zero)]
    for t in range(1, NY):
        same.append(jnp.where(seg[t] == seg[t - 1], one, zero))
    ends = [jnp.where(seg[t] == seg[NY - 1], one, zero) for t in range(NY)]
    starts = [jnp.where(seg[t] == seg[0], one, zero) for t in range(NY)]
    sub = lax.broadcasted_iota(jnp.int32, (8, CH), 0)

    def by_tile(values):
        total = jnp.full((8, CH), values[0], F32)
        for t in range(1, NY):
            total = jnp.where((sub >> 1) == t, values[t], total)
        return total

    joined = jnp.where((sub & 1) == 1, one, by_tile(same))
    subf = sub.astype(F32)
    rate8 = jnp.broadcast_to(rate[:, None, :], (MODES, 8, CH))
    gain8 = jnp.broadcast_to(gain[:, None, :], (MODES, 8, CH))
    dtab[...] = jnp.exp(-rate8)
    gtab[...] = gain8
    atab[...] = jnp.exp(-rate8 * (CHUNK * (7.0 - subf))[None]) * by_tile(ends)[None]
    ctab[...] = gain8 * jnp.exp(-rate8 * (CHUNK * subf)[None]) * by_tile(starts)[None]
    chunk_decay = jnp.exp(-rate8 * float(CHUNK)) * joined[None]

    w_place(1)

    streams = (fq, fk, fv)
    here = pl.multiple_of(8 + y * TILE, 8)
    for s in range(3):
        streams[s][pl.ds(here, TILE)] = stage[y, s].astype(F32)
    for j in range(1, NY):
        y_copies[j - 1].wait_recv()
        origin = lax.rem(y - j + NY, NY)
        at = pl.multiple_of(8 + origin * TILE, 8)
        for s in range(3):
            streams[s][pl.ds(at, TILE)] = rbuf[origin, s].astype(F32)
    @pl.when(z > 0)
    def _():
        rim_copy(0).wait_recv()

    for s in range(3):
        streams[s][0:8] = rim[s].astype(F32)[8:16]

    def load(s, b):
        return streams[s][pl.ds(8 + b, 8, stride=CHUNK), :]

    def mix(now, last, older):
        out = []
        for s in range(3):
            out.append(now[s] * taps[s][0] + last[s] * taps[s][1] + older[s] * taps[s][2])
        return out[0], (out[1] * out[2]).astype(BF).astype(F32)

    def keep(b, mixed):
        qs[b] = mixed[0]
        xs[b] = mixed[1]
        return mixed[1]

    m2 = [load(s, -2) * joined for s in range(3)]
    m1 = [load(s, -1) * joined for s in range(3)]
    f0 = [load(s, 0) for s in range(3)]
    f1 = [load(s, 1) for s in range(3)]
    d16 = dtab[...]
    x0 = keep(0, mix(f0, m1, m2))
    x1 = keep(1, mix(f1, f0, m1))
    h = x0[None] * d16 + x1[None]

    def first_pass(b, carry):
        h, last, older = carry
        now = [load(s, b) for s in range(3)]
        xb = keep(b, mix(now, last, older))
        return (h * dtab[...] + xb[None], now, last)

    h, _, _ = lax.fori_loop(2, CHUNK, first_pass, (h, f1, f0), unroll=2)

    asend[...] = jnp.sum(h * atab[...], axis=1).astype(BF)
    a_copies = []
    for k in range(1, BACK + 1):
        cp = pltpu.make_async_remote_copy(
            src_ref=asend, dst_ref=arecv.at[k - 1], send_sem=a_send.at[k - 1],
            recv_sem=a_recv.at[k - 1], device_id=dev(dz=k), device_id_type=MESH)
        a_copies.append(cp)

    for k in range(1, BACK + 1):
        @pl.when(z + k < NZ)
        def _():
            a_copies[k - 1].start()


    w_place(2)

    span = 1
    factor = chunk_decay
    state = h
    while span < 8:
        state = state + jnp.where(sub[None] >= span, factor * pltpu.roll(state, span, 1), zero)
        factor = factor * pltpu.roll(factor, span, 1)
        span *= 2
    entering = jnp.where(sub[None] >= 1, pltpu.roll(state, 1, 1) * joined[None], zero)

    def second_pass(b, h):
        xb = xs[b]
        h = h * dtab[...] + xb[None]
        ys[b] = skip * xb + jnp.sum(h * gtab[...], axis=0)
        return h

    lax.fori_loop(0, CHUNK, second_pass, entering, unroll=2)

    w_place(3)

    carried = jnp.zeros((MODES, CH), F32)
    for k in range(1, BACK + 1):
        @pl.when(z >= k)
        def _():
            a_copies[k - 1].wait_recv()

        ending = seg_ref[jnp.maximum((z - k) * NY + NY - 1, 0)]
        live = jnp.where(jnp.logical_and(z >= k, ending == seg[0]), one, zero)
        weight = jnp.exp(-rate * float(ROWS * (k - 1))) * live
        carried = carried + weight * arecv[k - 1].astype(F32)

    def third_pass(b, e):
        e = e * dtab[...]
        long_out = (ys[b] + jnp.sum(e, axis=0)).astype(BF).astype(F32)
        gbuf[pl.ds(b, 8, stride=CHUNK), :] = qs[b] * long_out
        return e

    lax.fori_loop(0, CHUNK, third_pass, ctab[...] * carried[:, None, :], unroll=2)
    for part in range(2):
        for t in range(NY):
            xbuf[part, chan, t * CHUNK : (t + 1) * CHUNK] = gbuf[
                (2 * t + part) * CHUNK : (2 * t + part + 1) * CHUNK].astype(BF)

    x_moves = (dict(dx=2), dict(dx=1), dict(dx=-1), dict(dc=1))
    x_copies = []
    for part in range(2):
        for i, move in enumerate(x_moves):
            cp = pltpu.make_async_remote_copy(
                src_ref=xbuf.at[part, chan], dst_ref=xbuf.at[part, chan],
                send_sem=x_send.at[part, i], recv_sem=x_recv.at[part, i], device_id=dev(**move),
                device_id_type=MESH)
            cp.start()
            x_copies.append(cp)
    w_place(4)

    f_copies = []
    p_copies = []
    for part in range(2):
        for i, dx in ((1, -1), (2, 1), (0, 2)):
            x_copies[4 * part + i].wait_recv()
            slot = lax.rem(x + dx + NX, NX) * 2 + core
            cp = pltpu.make_async_remote_copy(
                src_ref=xbuf.at[part, slot], dst_ref=xbuf.at[part, slot],
                send_sem=f_send.at[part, i], recv_sem=f_recv.at[part, i], device_id=dev(dc=1),
                device_id_type=MESH)
            cp.start()
            f_copies.append(cp)
        if part == 0:
            w_place(5)
        x_copies[4 * part + 3].wait_recv()
        for i in range(3):
            f_copies[3 * part + i].wait_recv()
        if part == 0:
            for number in range(1, NZ):
                if number not in waited:
                    await_w(number).wait_recv()

        total = jnp.zeros((NY * CHUNK, 512), F32)
        for p in range(NX):
            left = jnp.concatenate([xbuf[part, 2 * p], xbuf[part, 2 * p + 1]], axis=1)
            right = wbuf[4 * p : 4 * p + 4].reshape(256, 512)
            total = total + jnp.dot(left, right, preferred_element_type=F32)
        sums[part] = total
        for j in (2, 1, 3):
            rows = pl.ds(pl.multiple_of(lax.rem(y + j, NY) * CHUNK, CHUNK), CHUNK)
            psend[part, j - 1] = sums[part, rows].astype(BF)
            cp = pltpu.make_async_remote_copy(
                src_ref=psend.at[part, j - 1], dst_ref=precv.at[part, j - 1],
                send_sem=p_send.at[part, j - 1], recv_sem=p_recv.at[part, j - 1],
                device_id=dev(dy=j), device_id_type=MESH)
            cp.start()
            p_copies.append(cp)

    for part in range(2):
        rows = pl.ds(pl.multiple_of(y * CHUNK, CHUNK), CHUNK)
        mine_out = slice(part * CHUNK, (part + 1) * CHUNK)
        own[mine_out] = sums[part, rows] + res_ref[mine_out].astype(F32)
    for part in range(2):
        mine_out = slice(part * CHUNK, (part + 1) * CHUNK)
        for j in range(3):
            p_copies[3 * part + j].wait_recv()
        out_ref[mine_out] = (
            own[mine_out] + precv[part, 0].astype(F32) + precv[part, 1].astype(F32)
            + precv[part, 2].astype(F32)
        ).astype(BF)

    for cp in y_copies + x_copies + f_copies + p_copies:
        cp.wait_send()
    for number in range(1, NZ):
        await_w(number).wait_send()
    for k in range(1, BACK + 1):
        @pl.when(z + k < NZ)
        def _():
            a_copies[k - 1].wait_send()

    @pl.when(jnp.logical_and(y == NY - 1, z < NZ - 1))
    def _():
        for t in range(NY):
            rim_copy(t).wait_send()


def per_device(
    query, key, value, residual, short_taps, decay, residue, skip_gain, segments, out_weight
):
    vmem = pl.BlockSpec(memory_space=pltpu.VMEM)
    hbm = pl.BlockSpec(memory_space=pltpu.HBM)
    smem = pl.BlockSpec(memory_space=pltpu.SMEM)
    dma = pltpu.SemaphoreType.DMA
    scratch = [
        pltpu.VMEM((3 * TILE, 512), BF),
        pltpu.VMEM((TILE, 512), BF),
        pltpu.VMEM((3, 3, 512), F32),
        pltpu.VMEM((MODES, 512), F32),
        pltpu.VMEM((MODES, 512), F32),
        pltpu.VMEM((1, 512), F32),
        pltpu.VMEM((64, 512), BF),
        pltpu.VMEM((NY, 3, TILE, CH), BF),
        pltpu.VMEM((NY, 3, TILE, CH), BF),
        pltpu.VMEM((3, 16, CH), BF),
        pltpu.VMEM((8 + ROWS, CH), F32),
        pltpu.VMEM((8 + ROWS, CH), F32),
        pltpu.VMEM((8 + ROWS, CH), F32),
        pltpu.VMEM((48, 512), F32),
        pltpu.VMEM((CHUNK, 8, CH), F32),
        pltpu.VMEM((CHUNK, 8, CH), F32),
        pltpu.VMEM((CHUNK, 8, CH), F32),
        pltpu.VMEM((MODES, 8, CH), F32),
        pltpu.VMEM((MODES, 8, CH), F32),
        pltpu.VMEM((MODES, 8, CH), F32),
        pltpu.VMEM((MODES, 8, CH), F32),
        pltpu.VMEM((MODES, CH), BF),
        pltpu.VMEM((BACK, MODES, CH), BF),
        pltpu.VMEM((ROWS, CH), F32),
        pltpu.VMEM((2, 2 * NX, ROWS // 2, CH), BF),
        pltpu.VMEM((NZ, 64, 512), BF),
        pltpu.VMEM((2, NY - 1, CHUNK, 512), BF),
        pltpu.VMEM((2, NY - 1, CHUNK, 512), BF),
        pltpu.VMEM((TILE, 512), F32),
        pltpu.VMEM((2, ROWS // 2, 512), F32),
        dma((3,)), dma((3,)), dma((NY,)), dma,
        dma((BACK,)), dma((BACK,)), dma((2, 4)), dma((2, 4)), dma((2, 3)), dma((2, 3)),
        dma((15,)), dma((NZ,)), dma((2, 3)), dma((2, 3)), dma((9,)),
        pltpu.SemaphoreType.REGULAR, pltpu.SemaphoreType.REGULAR,
        pltpu.SemaphoreType.REGULAR, pltpu.SemaphoreType.REGULAR,
    ]
    return pl.pallas_call(
        kernel,
        out_shape=jax.ShapeDtypeStruct((TILE, 512), BF),
        in_specs=[smem] + [hbm] * 9,
        out_specs=vmem,
        scratch_shapes=scratch,
        compiler_params=pltpu.CompilerParams(
            collective_id=0, has_side_effects=True, vmem_limit_bytes=60 * 1024 * 1024),
        name="hyena_block",
    )(segments, query, key, value, residual, short_taps, decay, residue,
      skip_gain.reshape(1, -1), out_weight)


def solution(mesh):
    placed = (
        P("seq", "chan"), P("seq", "chan"), P("seq", "chan"), P("seq", "chan"),
        P(None, None, "chan"), P(None, "chan"), P(None, "chan"), P("chan"), P(),
        P("seq", "chan"),
    )
    return jax.shard_map(
        per_device, mesh=mesh, in_specs=placed, out_specs=P("seq", "chan"), check_vma=False
    )
```

```python
import jax
import jax.numpy as jnp
from jax import lax
from jax.experimental import pallas as pl
from jax.experimental.pallas import tpu as pltpu
from jax.sharding import PartitionSpec as P

MESH = pl.DeviceIdType.MESH
BF = jnp.bfloat16
F32 = jnp.float32

NZ, NY, NX = 16, 4, 4
TILE = 128
MODES = 16
CH = 128
ROWS = NY * TILE
CHUNK = ROWS // 8
BACK = 8

STEPS = (
    ((0, (2, -2)),),
    ((14, (2,)), (2, (-2,))),
    ((12, (2,)), (4, (-2,))),
    ((10, (2,)), (6, ())),
    ((0, (1, -1)),),
    ((14, (1,)), (2, (-1,))),
    ((12, (1,)), (4, (-1,))),
    ((10, (1,)), (6, (-1,))),
)
LATE = {1: (1, 4), 2: (2, 5, 6), 3: (3, 7)}
EARLY = {1: (1,), 3: (2, 6, 4, 5), 4: (3, 7)}


def kernel(
    seg_ref, q_hbm, k_hbm, v_hbm, res_hbm, taps_hbm, decay_hbm, residue_hbm, skip_hbm, w_hbm,
    out_hbm,
    out_ref, qkv, res_ref, taps_ref, decay_ref, residue_ref, skip_ref, w_ref,
    stage, rbuf, rim, fq, fk, fv, prm, xs, qs, ys, dtab, gtab, atab, ctab, asend, arecv,
    gbuf, xbuf, wbuf, psend, precv, own, sums,
    y_send, y_recv, rim_send, rim_recv, a_send, a_recv, x_send, x_recv, f_send, f_recv,
    w_send, w_recv, p_send, p_recv, in_sem, out_sem, go, zgo, blocks, plane,
):
    inputs = [
        pltpu.make_async_copy(there, ref, in_sem.at[i])
        for i, (there, ref) in enumerate((
            (w_hbm, w_ref), (q_hbm, qkv.at[0:TILE]), (k_hbm, qkv.at[TILE : 2 * TILE]),
            (v_hbm, qkv.at[2 * TILE : 3 * TILE]), (decay_hbm, decay_ref),
            (residue_hbm, residue_ref), (taps_hbm, taps_ref), (skip_hbm, skip_ref),
            (res_hbm, res_ref)))
    ]
    inputs[0].start()

    seq = lax.axis_index("seq")
    chan = lax.axis_index("chan")
    z, y = seq // NY, seq % NY
    x, core = chan // 2, chan % 2

    def dev(dz=0, dy=0, dx=0, dc=0, toy=None):
        yy = lax.rem(y + dy + NY, NY) if toy is None else toy
        return (
            lax.rem(z + dz + NZ, NZ) * NY + yy,
            lax.rem(x + dx + NX, NX) * 2 + (core if dc == 0 else 1 - core),
        )

    barrier = pltpu.get_barrier_semaphore()
    hub = y == 0
    hub_pair = y == 1

    def greet(sem, where):
        pl.semaphore_signal(sem, inc=1, device_id=where, device_id_type=MESH)

    arecv[...] = jnp.zeros_like(arecv)
    rim[...] = jnp.zeros_like(rim)

    @pl.when(hub)
    def _():
        for j in range(1, 2 * NX):
            greet(barrier, (z * NY, lax.rem(chan + j, 2 * NX)))
        for j in range(NZ):
            greet(barrier, dev(dz=j, toy=1))

    @pl.when(jnp.logical_not(hub))
    def _():
        greet(barrier, dev(toy=0))
        for j in range(1, NZ):
            greet(barrier, dev(dz=j))

    @pl.when(y != NY - 1)
    def _():
        greet(barrier, dev(dz=-1, toy=NY - 1))

    for cp in inputs[1:]:
        cp.start()

    def send_w(source, tile, dz, number):
        at = (number - 1) % NZ
        pltpu.make_async_remote_copy(
            src_ref=source, dst_ref=wbuf.at[tile], send_sem=w_send.at[at],
            recv_sem=w_recv.at[number], device_id=dev(dz=dz), device_id_type=MESH).start()

    def await_w(number):
        return pltpu.make_async_remote_copy(
            src_ref=w_ref, dst_ref=wbuf.at[lax.rem(z + number, NZ)], send_sem=w_send.at[number - 1],
            recv_sem=w_recv.at[number], device_id=dev(dz=1), device_id_type=MESH)

    def planes():
        @pl.when(jnp.logical_not(hub))
        def _():
            pl.semaphore_wait(
                barrier, 15 + jnp.where(hub_pair, 16, jnp.where(y == NY - 1, 3, 0)))

        @pl.when(hub_pair)
        def _():
            greet(zgo, dev(toy=0))

        @pl.when(hub)
        def _():
            pl.semaphore_wait(zgo, 1)

    late = z >= NZ // 2
    waited = (14, 2, 12, 4, 10, 6)

    def pass_on(step):
        for number, moves in STEPS[step]:
            tile = lax.rem(z + number, NZ)
            if 0 < step < 4:
                await_w(number).wait_recv()
            for dz in moves:
                send_w(wbuf.at[tile] if number else w_ref, tile, dz, (number - dz) % NZ)

    def w_place(place):
        for when, steps in ((late, LATE), (jnp.logical_not(late), EARLY)):
            if place in steps:
                @pl.when(when)
                def _():
                    for step in steps[place]:
                        pass_on(step)

    src = lax.broadcasted_iota(jnp.int32, (512, 512), 0)
    dst = lax.broadcasted_iota(jnp.int32, (512, 512), 1)
    wanted = ((dst >> 6) & 1) * 256 + (dst >> 7) * 64 + (dst & 63)
    perm = jnp.where(src == wanted, 1.0, 0.0).astype(BF)

    @pl.when(hub)
    def _():
        pl.semaphore_wait(barrier, NY - 1 + 2 * NX - 1)
        for j in range(1, NY):
            greet(go, dev(toy=j))
        for j in range(1, 2 * NX):
            greet(blocks, (z * NY, lax.rem(chan + j, 2 * NX)))

    inputs[0].wait()

    @pl.when(late)
    def _():
        planes()
        pass_on(0)

    for i in range(1, 4):
        inputs[i].wait()
    moved = jnp.dot(qkv[...], perm, preferred_element_type=F32).astype(BF)
    for s in range(3):
        for t in range(NY):
            stage[t, s] = moved[s * TILE : (s + 1) * TILE, t * CH : (t + 1) * CH]

    @pl.when(jnp.logical_not(hub))
    def _():
        pl.semaphore_wait(go, 1)

    y_copies = []
    for group, of in enumerate((slice(1, 3), slice(0, 1))):
        for j in range(1, NY):
            to = lax.rem(y + j, NY)
            cp = pltpu.make_async_remote_copy(
                src_ref=stage.at[to, of], dst_ref=rbuf.at[y, of], send_sem=y_send.at[group, j - 1],
                recv_sem=y_recv.at[group, j - 1], device_id=dev(dy=j), device_id_type=MESH)
            cp.start()
            y_copies.append(cp)

    def rim_copy(t):
        return pltpu.make_async_remote_copy(
            src_ref=stage.at[t, :, pl.ds(TILE - 16, 16), :], dst_ref=rim, send_sem=rim_send.at[t],
            recv_sem=rim_recv, device_id=dev(dz=1, toy=t), device_id_type=MESH)

    @pl.when(jnp.logical_not(late))
    def _():
        planes()
        pass_on(0)

    @pl.when(jnp.logical_and(y == NY - 1, z < NZ - 1))
    def _():
        for t in range(NY):
            rim_copy(t).start()

    @pl.when(hub)
    def _():
        pl.semaphore_wait(blocks, 2 * NX - 1)
        for j in range(1, NY):
            greet(plane, dev(toy=j))

    @pl.when(jnp.logical_not(hub))
    def _():
        pl.semaphore_wait(plane, 1)

    wbuf[z] = w_ref[...]

    for cp in inputs[4:]:
        cp.wait()
    prm[0:16] = decay_ref[...]
    prm[16:32] = residue_ref[...]
    for s in range(3):
        prm[32 + 3 * s : 35 + 3 * s] = taps_ref[s]
    prm[41:42] = skip_ref[...]
    prm[42:48] = jnp.zeros((6, 512), F32)
    lane = lax.broadcasted_iota(jnp.int32, (512, CH), 1)
    row = lax.broadcasted_iota(jnp.int32, (512, CH), 0)
    pick = jnp.where(row == ((lane >> 6) & 1) * 256 + y * 64 + (lane & 63), 1.0, 0.0).astype(F32)
    mine = jnp.dot(
        prm[...], pick, precision=lax.Precision.HIGHEST, preferred_element_type=F32)
    rate = mine[0:16]
    gain = mine[16:32] * jnp.sqrt(rate)
    taps = [[jnp.broadcast_to(mine[32 + 3 * s + j : 33 + 3 * s + j], (8, CH)) for j in range(3)]
            for s in range(3)]
    skip = jnp.broadcast_to(mine[41:42], (8, CH))

    one = jnp.float32(1.0)
    zero = jnp.float32(0.0)
    seg = [seg_ref[z * NY + t] for t in range(NY)]
    before = seg_ref[jnp.maximum(z * NY - 1, 0)]
    same = [jnp.where(jnp.logical_and(z > 0, before == seg[0]), one, zero)]
    for t in range(1, NY):
        same.append(jnp.where(seg[t] == seg[t - 1], one, zero))
    ends = [jnp.where(seg[t] == seg[NY - 1], one, zero) for t in range(NY)]
    starts = [jnp.where(seg[t] == seg[0], one, zero) for t in range(NY)]
    sub = lax.broadcasted_iota(jnp.int32, (8, CH), 0)

    def by_tile(values):
        total = jnp.full((8, CH), values[0], F32)
        for t in range(1, NY):
            total = jnp.where((sub >> 1) == t, values[t], total)
        return total

    joined = jnp.where((sub & 1) == 1, one, by_tile(same))
    subf = sub.astype(F32)
    rate8 = jnp.broadcast_to(rate[:, None, :], (MODES, 8, CH))
    gain8 = jnp.broadcast_to(gain[:, None, :], (MODES, 8, CH))
    dtab[...] = jnp.exp(-rate8)
    gtab[...] = gain8
    atab[...] = jnp.exp(-rate8 * (CHUNK * (7.0 - subf))[None]) * by_tile(ends)[None]
    ctab[...] = gain8 * jnp.exp(-rate8 * (CHUNK * subf)[None]) * by_tile(starts)[None]
    chunk_decay = jnp.exp(-rate8 * float(CHUNK)) * joined[None]

    w_place(1)

    streams = (fq, fk, fv)

    def fill(group, of):
        here = pl.multiple_of(8 + y * TILE, 8)
        for s in of:
            streams[s][pl.ds(here, TILE)] = stage[y, s].astype(F32)
        for j in range(1, NY):
            y_copies[group * (NY - 1) + j - 1].wait_recv()
            origin = lax.rem(y - j + NY, NY)
            at = pl.multiple_of(8 + origin * TILE, 8)
            for s in of:
                streams[s][pl.ds(at, TILE)] = rbuf[origin, s].astype(F32)

    fill(0, (1, 2))

    @pl.when(z > 0)
    def _():
        rim_copy(0).wait_recv()

    for s in range(3):
        streams[s][0:8] = rim[s].astype(F32)[8:16]

    def load(s, b):
        return streams[s][pl.ds(8 + b, 8, stride=CHUNK), :]

    def short(s, now, last, older):
        return now * taps[s][0] + last * taps[s][1] + older * taps[s][2]

    def start(of):
        return (
            [load(s, -2) * joined for s in of], [load(s, -1) * joined for s in of],
            [load(s, 0) for s in of], [load(s, 1) for s in of])

    def mix(b, now, last, older):
        ks = short(1, now[0], last[0], older[0])
        vs = short(2, now[1], last[1], older[1])
        xb = (ks * vs).astype(BF).astype(F32)
        xs[b] = xb
        return xb

    m2, m1, f0, f1 = start((1, 2))
    h = mix(0, f0, m1, m2)[None] * dtab[...] + mix(1, f1, f0, m1)[None]

    def first_pass(b, carry):
        h, last, older = carry
        now = [load(s, b) for s in (1, 2)]
        xb = mix(b, now, last, older)
        return (h * dtab[...] + xb[None], now, last)

    h, _, _ = lax.fori_loop(2, CHUNK, first_pass, (h, f1, f0), unroll=2)

    asend[...] = jnp.sum(h * atab[...], axis=1).astype(BF)
    a_copies = []
    for k in range(1, BACK + 1):
        cp = pltpu.make_async_remote_copy(
            src_ref=asend, dst_ref=arecv.at[k - 1], send_sem=a_send.at[k - 1],
            recv_sem=a_recv.at[k - 1], device_id=dev(dz=k), device_id_type=MESH)
        a_copies.append(cp)

    for k in range(1, BACK + 1):
        @pl.when(z + k < NZ)
        def _():
            a_copies[k - 1].start()


    w_place(2)

    span = 1
    factor = chunk_decay
    state = h
    while span < 8:
        state = state + jnp.where(sub[None] >= span, factor * pltpu.roll(state, span, 1), zero)
        factor = factor * pltpu.roll(factor, span, 1)
        span *= 2
    entering = jnp.where(sub[None] >= 1, pltpu.roll(state, 1, 1) * joined[None], zero)

    fill(1, (0,))
    m2, m1, f0, f1 = start((0,))

    def convolve(b, h, now, last, older):
        qs[b] = short(0, now, last, older)
        xb = xs[b]
        h = h * dtab[...] + xb[None]
        ys[b] = skip * xb + jnp.sum(h * gtab[...], axis=0)
        return h

    h = convolve(0, entering, f0[0], m1[0], m2[0])
    h = convolve(1, h, f1[0], f0[0], m1[0])

    def second_pass(b, carry):
        h, last, older = carry
        now = load(0, b)
        return (convolve(b, h, now, last, older), now, last)

    lax.fori_loop(2, CHUNK, second_pass, (h, f1[0], f0[0]), unroll=2)

    w_place(3)

    carried = jnp.zeros((MODES, CH), F32)
    for k in range(1, BACK + 1):
        @pl.when(z >= k)
        def _():
            a_copies[k - 1].wait_recv()

        ending = seg_ref[jnp.maximum((z - k) * NY + NY - 1, 0)]
        live = jnp.where(jnp.logical_and(z >= k, ending == seg[0]), one, zero)
        weight = jnp.exp(-rate * float(ROWS * (k - 1))) * live
        carried = carried + weight * arecv[k - 1].astype(F32)

    w_place(35)
    def third_pass(b, e):
        e = e * dtab[...]
        long_out = (ys[b] + jnp.sum(e, axis=0)).astype(BF).astype(F32)
        gbuf[pl.ds(b, 8, stride=CHUNK), :] = qs[b] * long_out
        return e

    lax.fori_loop(0, CHUNK, third_pass, ctab[...] * carried[:, None, :], unroll=2)
    for part in range(2):
        for t in range(NY):
            xbuf[part, chan, t * CHUNK : (t + 1) * CHUNK] = gbuf[
                (2 * t + part) * CHUNK : (2 * t + part + 1) * CHUNK].astype(BF)

    x_moves = (dict(dx=2), dict(dx=1), dict(dx=-1), dict(dc=1))
    x_copies = []
    for part in range(2):
        for i, move in enumerate(x_moves):
            cp = pltpu.make_async_remote_copy(
                src_ref=xbuf.at[part, chan], dst_ref=xbuf.at[part, chan],
                send_sem=x_send.at[part, i], recv_sem=x_recv.at[part, i], device_id=dev(**move),
                device_id_type=MESH)
            cp.start()
            x_copies.append(cp)
    w_place(4)

    f_copies = []
    p_copies = []
    for part in range(2):
        for i, dx in ((1, -1), (2, 1), (0, 2)):
            x_copies[4 * part + i].wait_recv()
            slot = lax.rem(x + dx + NX, NX) * 2 + core
            cp = pltpu.make_async_remote_copy(
                src_ref=xbuf.at[part, slot], dst_ref=xbuf.at[part, slot],
                send_sem=f_send.at[part, i], recv_sem=f_recv.at[part, i], device_id=dev(dc=1),
                device_id_type=MESH)
            cp.start()
            f_copies.append(cp)
        if part == 0:
            w_place(5)
        x_copies[4 * part + 3].wait_recv()
        for i in range(3):
            f_copies[3 * part + i].wait_recv()
        if part == 0:
            for number in range(1, NZ):
                if number not in waited:
                    await_w(number).wait_recv()

        total = jnp.zeros((NY * CHUNK, 512), F32)
        for p in range(NX):
            left = jnp.concatenate([xbuf[part, 2 * p], xbuf[part, 2 * p + 1]], axis=1)
            right = wbuf[4 * p : 4 * p + 4].reshape(256, 512)
            total = total + jnp.dot(left, right, preferred_element_type=F32)
        sums[part] = total
        for j in (2, 1, 3):
            rows = pl.ds(pl.multiple_of(lax.rem(y + j, NY) * CHUNK, CHUNK), CHUNK)
            psend[part, j - 1] = sums[part, rows].astype(BF)
            cp = pltpu.make_async_remote_copy(
                src_ref=psend.at[part, j - 1], dst_ref=precv.at[part, j - 1],
                send_sem=p_send.at[part, j - 1], recv_sem=p_recv.at[part, j - 1],
                device_id=dev(dy=j), device_id_type=MESH)
            cp.start()
            p_copies.append(cp)

    for part in range(2):
        rows = pl.ds(pl.multiple_of(y * CHUNK, CHUNK), CHUNK)
        mine_out = slice(part * CHUNK, (part + 1) * CHUNK)
        own[mine_out] = sums[part, rows] + res_ref[mine_out].astype(F32)
    outputs = []
    for part in range(2):
        mine_out = slice(part * CHUNK, (part + 1) * CHUNK)
        for j in range(3):
            p_copies[3 * part + j].wait_recv()
        out_ref[mine_out] = (
            own[mine_out] + precv[part, 0].astype(F32) + precv[part, 1].astype(F32)
            + precv[part, 2].astype(F32)
        ).astype(BF)
        outputs.append(pltpu.make_async_copy(
            out_ref.at[mine_out], out_hbm.at[mine_out], out_sem.at[part]))
        outputs[part].start()

    for cp in outputs:
        cp.wait()
    for cp in y_copies + x_copies + f_copies + p_copies:
        cp.wait_send()
    for number in range(1, NZ):
        await_w(number).wait_send()
    for k in range(1, BACK + 1):
        @pl.when(z + k < NZ)
        def _():
            a_copies[k - 1].wait_send()

    @pl.when(jnp.logical_and(y == NY - 1, z < NZ - 1))
    def _():
        for t in range(NY):
            rim_copy(t).wait_send()


def per_device(
    query, key, value, residual, short_taps, decay, residue, skip_gain, segments, out_weight
):
    vmem = pl.BlockSpec(memory_space=pltpu.VMEM)
    hbm = pl.BlockSpec(memory_space=pltpu.HBM)
    smem = pl.BlockSpec(memory_space=pltpu.SMEM)
    dma = pltpu.SemaphoreType.DMA
    scratch = [
        pltpu.VMEM((TILE, 512), BF),
        pltpu.VMEM((3 * TILE, 512), BF),
        pltpu.VMEM((TILE, 512), BF),
        pltpu.VMEM((3, 3, 512), F32),
        pltpu.VMEM((MODES, 512), F32),
        pltpu.VMEM((MODES, 512), F32),
        pltpu.VMEM((1, 512), F32),
        pltpu.VMEM((64, 512), BF),
        pltpu.VMEM((NY, 3, TILE, CH), BF),
        pltpu.VMEM((NY, 3, TILE, CH), BF),
        pltpu.VMEM((3, 16, CH), BF),
        pltpu.VMEM((8 + ROWS + CHUNK, CH), F32),
        pltpu.VMEM((8 + ROWS + CHUNK, CH), F32),
        pltpu.VMEM((8 + ROWS + CHUNK, CH), F32),
        pltpu.VMEM((48, 512), F32),
        pltpu.VMEM((CHUNK, 8, CH), F32),
        pltpu.VMEM((CHUNK, 8, CH), F32),
        pltpu.VMEM((CHUNK, 8, CH), F32),
        pltpu.VMEM((MODES, 8, CH), F32),
        pltpu.VMEM((MODES, 8, CH), F32),
        pltpu.VMEM((MODES, 8, CH), F32),
        pltpu.VMEM((MODES, 8, CH), F32),
        pltpu.VMEM((MODES, CH), BF),
        pltpu.VMEM((BACK, MODES, CH), BF),
        pltpu.VMEM((ROWS + CHUNK, CH), F32),
        pltpu.VMEM((2, 2 * NX, ROWS // 2, CH), BF),
        pltpu.VMEM((NZ, 64, 512), BF),
        pltpu.VMEM((2, NY - 1, CHUNK, 512), BF),
        pltpu.VMEM((2, NY - 1, CHUNK, 512), BF),
        pltpu.VMEM((TILE, 512), F32),
        pltpu.VMEM((2, ROWS // 2, 512), F32),
        dma((2, 3)), dma((2, 3)), dma((NY,)), dma,
        dma((BACK,)), dma((BACK,)), dma((2, 4)), dma((2, 4)), dma((2, 3)), dma((2, 3)),
        dma((15,)), dma((NZ,)), dma((2, 3)), dma((2, 3)), dma((9,)), dma((2,)),
        pltpu.SemaphoreType.REGULAR, pltpu.SemaphoreType.REGULAR,
        pltpu.SemaphoreType.REGULAR, pltpu.SemaphoreType.REGULAR,
    ]
    return pl.pallas_call(
        kernel,
        out_shape=jax.ShapeDtypeStruct((TILE, 512), BF),
        in_specs=[smem] + [hbm] * 9,
        out_specs=hbm,
        scratch_shapes=scratch,
        compiler_params=pltpu.CompilerParams(
            collective_id=0, has_side_effects=True, vmem_limit_bytes=60 * 1024 * 1024),
        name="hyena_block",
    )(segments, query, key, value, residual, short_taps, decay, residue,
      skip_gain.reshape(1, -1), out_weight)


def solution(mesh):
    placed = (
        P("seq", "chan"), P("seq", "chan"), P("seq", "chan"), P("seq", "chan"),
        P(None, None, "chan"), P(None, "chan"), P(None, "chan"), P("chan"), P(),
        P("seq", "chan"),
    )
    return jax.shard_map(
        per_device, mesh=mesh, in_specs=placed, out_specs=P("seq", "chan"), check_vma=False
    )
```
